32 devices in a mesh: row: 2 (over y), col: 4 (over z), depth: 4 (over x, core).
Axes of the slice: x: 2, y: 2, z: 4, core: 2. Of those that a mesh axis runs over, the one named last changes fastest.
Arguments:
- tokens: bfloat16 [2048, 6144], P(('col', 'depth'), 'row'), may hold values from -6 to 6
- w_in: bfloat16 [6144, 12288], P('row', 'col'), may hold values from -0.078125 to 0.078125
- w_out: bfloat16 [12288, 6144], P('col', 'row'), may hold values from -0.0546875 to 0.0546875
- grad_out: bfloat16 [2048, 6144], P(('col', 'depth'), 'row'), may hold values from -1.5 to 1.5
Outputs:
- output: bfloat16 [2048, 6144], P(('col', 'depth'), 'row')
- grad_tokens: bfloat16 [2048, 6144], P(('col', 'depth'), 'row')
- grad_w_in: bfloat16 [6144, 12288], P('row', ('col', 'depth'))
- grad_w_out: bfloat16 [12288, 6144], P(('col', 'depth'), 'row')
The draws below stay inside these ranges and needn't reach their ends.
All inputs are finite; a program needn't handle non-finite values.
Results may differ from the reference program's by a relative error of at most 0.029.
Values may be sent and summed in bfloat16 or wider, within the bound.
A program may use at most 192 MiB of HBM per device.

```python
import jax
import jax.numpy as jnp
from jax import lax

D = 6144
FF = 12288
TOK_DEV = 128
TOKENS = 2048
N_COL = 4
N_DEPTH = 4


def shard_levels(own_key, dims, cuts, least, largest):
    def one(position, shards_of):
        heights = jax.random.uniform(jax.random.fold_in(jax.random.fold_in(own_key, 6), position), (shards_of,), jnp.float32, least / len(cuts), largest / len(cuts))
        return jnp.repeat(jnp.exp(heights), dims[position] // shards_of).reshape((-1,) + (1,) * (len(dims) - position - 1))

    factor_of = one(*cuts[0])
    for cut in cuts[1:]:
        factor_of = factor_of * one(*cut)
    return factor_of


def scatter_about(own_key, extent, scale, bound, split=(), held_as=jnp.bfloat16):
    entries = scale * jax.random.normal(own_key, extent, jnp.float32)
    if split:
        entries = entries * shard_levels(own_key, extent, split, -0.22, 0.18)
    return jnp.clip(entries, -bound, bound).astype(held_as)


def setup_inputs(seed: int = 0) -> dict:
    key_list = jax.random.split(jax.random.key(seed), 5)
    return {
        "tokens": scatter_about(key_list[0], (TOKENS, D), 1.0, 6.0, ((0, 16), (1, 2))),
        "w_in": scatter_about(key_list[1], (D, FF), D ** -0.5, 0.078125, ((0, 2), (1, 4))),
        "w_out": scatter_about(key_list[2], (FF, D), FF ** -0.5, 0.0546875, ((0, 4), (1, 2))),
        "grad_out": scatter_about(key_list[3], (TOKENS, D), 0.25, 1.5, ((0, 16), (1, 2))),
    }


def gelu_tanh(value):
    return jax.nn.gelu(value, approximate=True)

def reference(tokens, w_in, w_out, grad_out):
    pre = jnp.dot(tokens, w_in, preferred_element_type=jnp.float32)
    act_full, backward = jax.vjp(gelu_tanh, pre)
    act = act_full.astype(jnp.bfloat16)
    output = jnp.dot(act, w_out, preferred_element_type=jnp.float32).astype(jnp.bfloat16)
    grad_act = jnp.dot(grad_out, w_out.T, preferred_element_type=jnp.float32)
    grad_pre = backward(grad_act)[0].astype(jnp.bfloat16)
    grad_tokens = jnp.dot(grad_pre, w_in.T, preferred_element_type=jnp.float32).astype(jnp.bfloat16)

    def grouped(array):
        width = array.shape[1]
        shaped = array.reshape(N_COL, N_DEPTH, TOK_DEV, width)
        return jnp.transpose(shaped, (1, 0, 2, 3)).reshape(N_DEPTH, N_COL * TOK_DEV, width)

    def accumulate(carry, pieces):
        tok_g, gpre_g, act_g, gout_g = pieces
        part_in = lax.dot_general(tok_g, gpre_g, (((0,), (0,)), ((), ())), preferred_element_type=jnp.float32).astype(jnp.bfloat16)
        part_out = lax.dot_general(act_g, gout_g, (((0,), (0,)), ((), ())), preferred_element_type=jnp.float32).astype(jnp.bfloat16)
        part_in, part_out = lax.optimization_barrier((part_in, part_out))
        return ((carry[0] + part_in.astype(jnp.float32), carry[1] + part_out.astype(jnp.float32)), None)
    start = (jnp.zeros((D, FF), jnp.float32), jnp.zeros((FF, D), jnp.float32))
    sums, _ = lax.scan(accumulate, start, (grouped(tokens), grouped(grad_pre), grouped(act), grouped(grad_out)))
    return (output, grad_tokens, sums[0].astype(jnp.bfloat16), sums[1].astype(jnp.bfloat16))
```

```python
import jax
import jax.numpy as jnp
from jax import lax
from jax.sharding import PartitionSpec as P

CHUNKS = 2


def gelu_tanh(value):
    return jax.nn.gelu(value, approximate=True)


def dot(a, b, ca, cb):
    return lax.dot_general(
        a, b, (((ca,), (cb,)), ((), ())), preferred_element_type=jnp.float32
    )


def line_gather(block, n):
    right = left = block
    rights, lefts = [block], [block]
    for step in range(1, n):
        right = lax.ppermute(right, "col", [(c, c + 1) for c in range(step - 1, n - 1)])
        left = lax.ppermute(left, "col", [(c, c - 1) for c in range(1, n - step + 1)])
        rights.append(right)
        lefts.append(left)
    me = lax.axis_index("col")
    slots = [block]
    for k in range(1, n):
        slots.append(jnp.where(me + k < n, lefts[k], rights[n - k]))
    return slots


def line_reduce(parts, n):
    if n == 1:
        return parts[0]
    right = left = None
    for step in range(1, n):
        to_right, to_left = parts[n - step], parts[step]
        if right is not None:
            to_right = (to_right.astype(jnp.float32) + right.astype(jnp.float32)).astype(
                jnp.bfloat16
            )
            to_left = (to_left.astype(jnp.float32) + left.astype(jnp.float32)).astype(
                jnp.bfloat16
            )
        right = lax.ppermute(to_right, "col", [(c, c + 1) for c in range(step)])
        left = lax.ppermute(to_left, "col", [(c, c - 1) for c in range(n - step, n)])
    total = parts[0].astype(jnp.float32) + right.astype(jnp.float32) + left.astype(jnp.float32)
    return total.astype(jnp.bfloat16)


def row_sum(part, n):
    total = part.astype(jnp.float32)
    for step in range(1, n):
        other = lax.ppermute(part, "row", [(r, (r + step) % n) for r in range(n)])
        total = total + other.astype(jnp.float32)
    return total


def depth_masks(n):
    masks = [0]
    bit = n // 2
    while bit:
        masks = masks + [m ^ bit for m in masks]
        bit //= 2
    return masks


def depth_gather(mine, n):
    blocks = [mine]
    bit = n // 2
    while bit:
        blocks = blocks + [
            lax.ppermute(b, "depth", [(d, d ^ bit) for d in range(n)]) for b in blocks
        ]
        bit //= 2
    return blocks


def depth_exchange(mine, n):
    me = lax.axis_index("depth")
    width = mine.shape[1] // n
    out = []
    for m in depth_masks(n):
        piece = lax.dynamic_slice_in_dim(mine, (me ^ m) * width, width, axis=1)
        if m:
            piece = lax.ppermute(piece, "depth", [(d, d ^ m) for d in range(n)])
        out.append(piece)
    return out


def body(n_row, n_col, n_depth, tokens, w_in, w_out, grad_out):
    rows = tokens.shape[0] // CHUNKS
    cut = lambda a, j: a[j * rows : (j + 1) * rows]

    def gathered(a):
        return [
            jnp.concatenate(line_gather(cut(a, j), n_col), axis=0) for j in range(CHUNKS)
        ]

    def reduced(part):
        return line_reduce([cut(part, k) for k in range(n_col)], n_col)

    toks = gathered(tokens)
    grads = gathered(grad_out)
    acts, pulls = [], []
    for tok in toks:
        pre = row_sum(dot(tok, w_in, 1, 0).astype(jnp.bfloat16), n_row)
        act, pull = jax.vjp(gelu_tanh, pre)
        acts.append(act.astype(jnp.bfloat16))
        pulls.append(pull)
    gpres = []
    for grad, pull in zip(grads, pulls):
        gact = row_sum(dot(grad, w_out, 1, 1).astype(jnp.bfloat16), n_row)
        gpres.append(pull(gact)[0].astype(jnp.bfloat16))
    outs = [reduced(dot(act, w_out, 1, 0).astype(jnp.bfloat16)) for act in acts]
    gtoks = [reduced(dot(gpre, w_in, 1, 1).astype(jnp.bfloat16)) for gpre in gpres]

    def spread(pieces, fetch):
        return jnp.concatenate([b for p in pieces for b in fetch(p, n_depth)], axis=0)

    all_tok = spread(toks, depth_gather)
    all_grad = spread(grads, depth_gather)
    all_act = spread(acts, depth_exchange)
    all_gpre = spread(gpres, depth_exchange)
    grad_w_out = dot(all_act, all_grad, 0, 0).astype(jnp.bfloat16)
    grad_w_in = dot(all_tok, all_gpre, 0, 0).astype(jnp.bfloat16)
    return (
        jnp.concatenate(outs, axis=0),
        jnp.concatenate(gtoks, axis=0),
        grad_w_in,
        grad_w_out,
    )


def solution(mesh):
    placed = (
        P(("col", "depth"), "row"),
        P("row", "col"),
        P("col", "row"),
        P(("col", "depth"), "row"),
    )
    sizes = tuple(mesh.shape[a] for a in ("row", "col", "depth"))
    return jax.shard_map(
        lambda *args: body(*sizes, *args),
        mesh=mesh,
        in_specs=placed,
        out_specs=(
            P(("col", "depth"), "row"),
            P(("col", "depth"), "row"),
            P("row", ("col", "depth")),
            P(("col", "depth"), "row"),
        ),
        check_vma=False,
    )
```

```python
import jax
import jax.numpy as jnp
from jax import lax
from jax.sharding import PartitionSpec as P


def gelu_tanh(value):
    return jax.nn.gelu(value, approximate=True)


def dot(a, b, ca, cb):
    return lax.dot_general(
        a, b, (((ca,), (cb,)), ((), ())), preferred_element_type=jnp.float32
    )


def line_gather(block, n):
    right = left = block
    rights, lefts = [block], [block]
    for step in range(1, n):
        right = lax.ppermute(right, "col", [(c, c + 1) for c in range(step - 1, n - 1)])
        left = lax.ppermute(left, "col", [(c, c - 1) for c in range(1, n - step + 1)])
        rights.append(right)
        lefts.append(left)
    me = lax.axis_index("col")
    slots = [block]
    for k in range(1, n):
        slots.append(jnp.where(me + k < n, lefts[k], rights[n - k]))
    return slots


def line_reduce(parts, n):
    if n == 1:
        return parts[0]
    right = left = None
    for step in range(1, n):
        to_right, to_left = parts[n - step], parts[step]
        if right is not None:
            to_right = (to_right.astype(jnp.float32) + right.astype(jnp.float32)).astype(
                jnp.bfloat16
            )
            to_left = (to_left.astype(jnp.float32) + left.astype(jnp.float32)).astype(
                jnp.bfloat16
            )
        right = lax.ppermute(to_right, "col", [(c, c + 1) for c in range(step)])
        left = lax.ppermute(to_left, "col", [(c, c - 1) for c in range(n - step, n)])
    total = parts[0].astype(jnp.float32) + right.astype(jnp.float32) + left.astype(jnp.float32)
    return total.astype(jnp.bfloat16)


def row_sum(part, n):
    total = part.astype(jnp.float32)
    for step in range(1, n):
        other = lax.ppermute(part, "row", [(r, (r + step) % n) for r in range(n)])
        total = total + other.astype(jnp.float32)
    return total


def depth_high(mine, n):
    blocks, masks = [mine], [0]
    bit = n // 2
    while bit > 1:
        blocks = blocks + [
            lax.ppermute(b, "depth", [(d, d ^ bit) for d in range(n)]) for b in blocks
        ]
        masks = masks + [m ^ bit for m in masks]
        bit //= 2
    return blocks, masks


def depth_exchange(mine, masks, n):
    me = lax.axis_index("depth")
    width = mine.shape[1] // n
    out = []
    for m in masks:
        piece = lax.dynamic_slice_in_dim(mine, (me ^ m) * width, width, axis=1)
        if m:
            piece = lax.ppermute(piece, "depth", [(d, d ^ m) for d in range(n)])
        out.append(piece)
    return out


def cat(*blocks):
    return jnp.concatenate(blocks, axis=0)


def body(n_row, n_col, n_depth, tokens, w_in, w_out, grad_out):
    rows = tokens.shape[0]
    half = n_col // 2
    tie = lax.optimization_barrier

    def fold(slots):
        return cat(*slots[0::2]), cat(*slots[1::2])

    def unfold(even, odd):
        slots = [None] * n_col
        slots[0::2] = [even[k * rows : (k + 1) * rows] for k in range(half)]
        slots[1::2] = [odd[k * rows : (k + 1) * rows] for k in range(half)]
        return slots

    def own_part(part):
        return part.astype(jnp.bfloat16)

    own_high, masks = depth_high(cat(tokens, grad_out), n_depth)
    all_masks = masks + [m ^ 1 for m in masks]

    tok_slots = line_gather(tokens, n_col)
    tok_even, tok_odd = fold(tok_slots)
    pre_even = row_sum(own_part(dot(tok_even, w_in, 1, 0)), n_row)
    grad_out, tok_odd, own_high = tie((grad_out, tok_odd, own_high))
    grad_slots = line_gather(grad_out, n_col)
    part_odd = own_part(dot(tok_odd, w_in, 1, 0))
    pre_odd = row_sum(part_odd, n_row)
    act_even, pull_even = jax.vjp(gelu_tanh, pre_even)
    act_odd, pull_odd = jax.vjp(gelu_tanh, pre_odd)
    act_even, act_odd = own_part(act_even), own_part(act_odd)

    tok_rest = cat(tok_even[rows:], tok_odd)
    tok_high, _ = depth_high(tok_rest, n_depth)
    grad_even, grad_odd = fold(grad_slots)
    grad_rest = cat(grad_even[rows:], grad_odd)
    grad_rest, tok_high = tie((grad_rest, tok_high))
    grad_high, _ = depth_high(grad_rest, n_depth)

    gact_odd_part = own_part(dot(grad_odd, w_out, 1, 1))
    gact_even_part = own_part(dot(grad_even, w_out, 1, 1))
    act_full, gact_odd_part, gact_even_part = tie(
        (cat(act_even, act_odd), gact_odd_part, gact_even_part)
    )
    gpre_odd = own_part(pull_odd(row_sum(gact_odd_part, n_row))[0])
    gpre_even = own_part(pull_even(row_sum(gact_even_part, n_row))[0])

    out_full = own_part(dot(act_full, w_out, 1, 0))
    output = line_reduce(unfold(out_full[: half * rows], out_full[half * rows :]), n_col)
    gtok_odd = own_part(dot(gpre_odd, w_in, 1, 1))
    gtok_even = own_part(dot(gpre_even, w_in, 1, 1))
    grad_tokens = line_reduce(unfold(gtok_even, gtok_odd), n_col)

    def spread(own, highs):
        high = cat(*[b for h, o in zip(highs, own) for b in (o, h)])
        return cat(high, lax.ppermute(high, "depth", [(d, d ^ 1) for d in range(n_depth)]))

    all_tok = spread([h[:rows] for h in own_high], tok_high)
    all_grad = spread([h[rows:] for h in own_high], grad_high)
    all_act = cat(*depth_exchange(act_full, all_masks, n_depth))
    gpre_high = zip(
        depth_exchange(gpre_even, all_masks, n_depth),
        depth_exchange(gpre_odd, all_masks, n_depth),
    )
    all_gpre = cat(*[b for pair in gpre_high for b in pair])
    all_act, gtok_even = tie((all_act, gtok_even))
    grad_w_out = own_part(dot(all_act, all_grad, 0, 0))
    grad_w_in = own_part(dot(all_tok, all_gpre, 0, 0))
    return output, grad_tokens, grad_w_in, grad_w_out


def solution(mesh):
    placed = (
        P(("col", "depth"), "row"),
        P("row", "col"),
        P("col", "row"),
        P(("col", "depth"), "row"),
    )
    sizes = tuple(mesh.shape[a] for a in ("row", "col", "depth"))
    return jax.shard_map(
        lambda *args: body(*sizes, *args),
        mesh=mesh,
        in_specs=placed,
        out_specs=(
            P(("col", "depth"), "row"),
            P(("col", "depth"), "row"),
            P("row", ("col", "depth")),
            P(("col", "depth"), "row"),
        ),
        check_vma=False,
    )
```

```python
import jax
import jax.numpy as jnp
from jax import lax
from jax.sharding import PartitionSpec as P


def gelu_tanh(value):
    return jax.nn.gelu(value, approximate=True)


def dot(a, b, ca, cb):
    return lax.dot_general(
        a, b, (((ca,), (cb,)), ((), ())), preferred_element_type=jnp.float32
    )


def line_gather(block, n, beside=()):
    right = left = block
    rights, lefts = [block], [block]
    me = lax.axis_index("col")
    slot = lambda k: jnp.where(me + k < n, lefts[k], rights[n - k])
    done = []
    for step in range(1, n):
        other = beside[step - 1](slot) if step <= len(beside) else None
        right = lax.ppermute(right, "col", [(c, c + 1) for c in range(step - 1, n - 1)])
        left = lax.ppermute(left, "col", [(c, c - 1) for c in range(1, n - step + 1)])
        if other is not None:
            right, left, other = lax.optimization_barrier((right, left, other))
        done.append(other)
        rights.append(right)
        lefts.append(left)
    return [block] + [slot(k) for k in range(1, n)], done


def line_reduce(parts, n, beside=None):
    if n == 1:
        return parts[0]
    right = left = None
    for step in range(1, n):
        to_right, to_left = parts[n - step], parts[step]
        if right is not None:
            to_right = (to_right.astype(jnp.float32) + right.astype(jnp.float32)).astype(
                jnp.bfloat16
            )
            to_left = (to_left.astype(jnp.float32) + left.astype(jnp.float32)).astype(
                jnp.bfloat16
            )
        right = lax.ppermute(to_right, "col", [(c, c + 1) for c in range(step)])
        left = lax.ppermute(to_left, "col", [(c, c - 1) for c in range(n - step, n)])
        if step == 1 and beside is not None:
            right, left, beside = lax.optimization_barrier((right, left, beside))
    total = parts[0].astype(jnp.float32) + right.astype(jnp.float32) + left.astype(jnp.float32)
    total = total.astype(jnp.bfloat16)
    return total if beside is None else (total, beside)


def row_sum(part, n):
    total = part.astype(jnp.float32)
    for step in range(1, n):
        other = lax.ppermute(part, "row", [(r, (r + step) % n) for r in range(n)])
        total = total + other.astype(jnp.float32)
    return total


def depth_masks(n):
    masks, bit = [0], n // 2
    while bit > 1:
        masks = masks + [m ^ bit for m in masks]
        bit //= 2
    return masks


def depth_high(mine, n):
    blocks, bit = [mine], n // 2
    while bit > 1:
        blocks = blocks + [
            lax.ppermute(b, "depth", [(d, d ^ bit) for d in range(n)]) for b in blocks
        ]
        bit //= 2
    return blocks


def high_columns(mine, masks, n):
    me = lax.axis_index("depth")
    width = 2 * mine.shape[1] // n
    out = []
    for m in masks:
        piece = lax.dynamic_slice_in_dim(mine, ((me ^ m) // 2) * width, width, axis=1)
        if m:
            piece = lax.ppermute(piece, "depth", [(d, d ^ m) for d in range(n)])
        out.append(piece)
    return out


def core_exchange(high, n):
    core = lax.axis_index("depth") % 2
    width = high.shape[1] // 2
    mine = lax.dynamic_slice_in_dim(high, core * width, width, axis=1)
    other = lax.dynamic_slice_in_dim(high, (1 - core) * width, width, axis=1)
    other = lax.ppermute(other, "depth", [(d, d ^ 1) for d in range(n)])
    first = core == 0
    return cat(jnp.where(first, mine, other), jnp.where(first, other, mine))


def core_gather(high, n):
    pairs = [[d, d + 1] for d in range(0, n, 2)]
    return lax.all_gather(high, "depth", axis=0, tiled=True, axis_index_groups=pairs)


def cat(*blocks):
    return jnp.concatenate(blocks, axis=0)


def body(n_row, n_col, n_depth, tokens, w_in, w_out, grad_out):
    rows = tokens.shape[0]
    half = n_col // 2
    tie = lax.optimization_barrier

    def fold(slots):
        return cat(*slots[0::2]), cat(*slots[1::2])

    def unfold(even, odd):
        slots = [None] * n_col
        slots[0::2] = [even[k * rows : (k + 1) * rows] for k in range(half)]
        slots[1::2] = [odd[k * rows : (k + 1) * rows] for k in range(half)]
        return slots

    def own_part(part):
        return part.astype(jnp.bfloat16)

    step_high = lambda block: depth_high(block, n_depth)
    masks = depth_masks(n_depth)

    tok_slots, tok_high = line_gather(
        tokens,
        n_col,
        [lambda slot: step_high(tokens), lambda slot: step_high(grad_out), lambda slot: step_high(slot(2))],
    )
    tok_own, grad_own, tok_two = tok_high
    tok_even, tok_odd = fold(tok_slots)
    pre_even = row_sum(own_part(dot(tok_even, w_in, 1, 0)), n_row)
    grad_out, tok_odd = tie((grad_out, tok_odd))
    tok_odd_high = step_high(tok_odd)
    part_odd = own_part(dot(tok_odd, w_in, 1, 0))
    pre_odd = row_sum(part_odd, n_row)
    grad_slots, grad_high = line_gather(
        grad_out, n_col, [lambda slot: None, lambda slot: None, lambda slot: step_high(slot(2))]
    )
    grad_two = grad_high[2]
    act_even, pull_even = jax.vjp(gelu_tanh, pre_even)
    act_odd, pull_odd = jax.vjp(gelu_tanh, pre_odd)
    act_even, act_odd = own_part(act_even), own_part(act_odd)
    grad_even, grad_odd = fold(grad_slots)
    grad_odd_high = step_high(grad_odd)

    out_even = own_part(dot(act_even, w_out, 1, 0))
    grad_even_in, out_even = tie((grad_even, out_even))
    gact_even = row_sum(own_part(dot(grad_even_in, w_out, 1, 1)), n_row)
    out_odd = own_part(dot(act_odd, w_out, 1, 0))
    grad_odd_in, out_odd = tie((grad_odd, out_odd))
    gact_odd = row_sum(own_part(dot(grad_odd_in, w_out, 1, 1)), n_row)
    output = line_reduce(unfold(out_even, out_odd), n_col)

    gpre_even = own_part(pull_even(gact_even)[0])
    gpre_odd = own_part(pull_odd(gact_odd)[0])
    gtok_even = own_part(dot(gpre_even, w_in, 1, 1))
    gtok_odd = own_part(dot(gpre_odd, w_in, 1, 1))

    def high_rows(own, two, odd_high, even, odd):
        blocks = [even, odd]
        for k in range(1, len(masks)):
            blocks += [own[k], two[k], odd_high[k]]
        return cat(*blocks)

    all_tok = core_gather(high_rows(tok_own, tok_two, tok_odd_high, tok_even, tok_odd), n_depth)
    all_grad = core_gather(
        high_rows(grad_own, grad_two, grad_odd_high, grad_even, grad_odd), n_depth
    )
    act_high = high_columns(cat(act_even, act_odd), masks, n_depth)
    all_act = core_exchange(cat(*act_high), n_depth)
    gpre_high = zip(
        high_columns(gpre_even, masks, n_depth), high_columns(gpre_odd, masks, n_depth)
    )
    all_gpre = core_exchange(cat(*[b for pair in gpre_high for b in pair]), n_depth)
    grad_w_out = own_part(dot(all_act, all_grad, 0, 0))
    grad_tokens, grad_w_out = line_reduce(unfold(gtok_even, gtok_odd), n_col, grad_w_out)
    grad_w_in = own_part(dot(all_tok, all_gpre, 0, 0))
    return output, grad_tokens, grad_w_in, grad_w_out


def solution(mesh):
    placed = (
        P(("col", "depth"), "row"),
        P("row", "col"),
        P("col", "row"),
        P(("col", "depth"), "row"),
    )
    sizes = tuple(mesh.shape[a] for a in ("row", "col", "depth"))
    return jax.shard_map(
        lambda *args: body(*sizes, *args),
        mesh=mesh,
        in_specs=placed,
        out_specs=(
            P(("col", "depth"), "row"),
            P(("col", "depth"), "row"),
            P("row", ("col", "depth")),
            P(("col", "depth"), "row"),
        ),
        check_vma=False,
    )
```

```python
import jax
import jax.numpy as jnp
from jax import lax
from jax.sharding import PartitionSpec as P


def gelu_tanh(value):
    return jax.nn.gelu(value, approximate=True)


def dot(a, b, ca, cb):
    return lax.dot_general(
        a, b, (((ca,), (cb,)), ((), ())), preferred_element_type=jnp.float32
    )


def line_gather(block, n, beside=()):
    right = left = block
    rights, lefts = [block], [block]
    me = lax.axis_index("col")
    slot = lambda k: jnp.where(me + k < n, lefts[k], rights[n - k])
    done = []
    for step in range(1, n):
        other = beside[step - 1](slot) if step <= len(beside) else None
        right = lax.ppermute(right, "col", [(c, c + 1) for c in range(step - 1, n - 1)])
        left = lax.ppermute(left, "col", [(c, c - 1) for c in range(1, n - step + 1)])
        if other is not None:
            right, left, other = lax.optimization_barrier((right, left, other))
        done.append(other)
        rights.append(right)
        lefts.append(left)
    return [block] + [slot(k) for k in range(1, n)], done


def line_reduce(parts, n, hooks):
    if n == 1:
        return parts(0)
    right = left = None
    for step in range(1, n):
        to_right, to_left = parts(n - step), parts(step)
        if right is not None:
            to_right = (to_right.astype(jnp.float32) + right.astype(jnp.float32)).astype(
                jnp.bfloat16
            )
            to_left = (to_left.astype(jnp.float32) + left.astype(jnp.float32)).astype(
                jnp.bfloat16
            )
        right = lax.ppermute(to_right, "col", [(c, c + 1) for c in range(step)])
        left = lax.ppermute(to_left, "col", [(c, c - 1) for c in range(n - step, n)])
        if step in hooks:
            right, left = hooks[step](right, left)
    total = parts(0).astype(jnp.float32) + right.astype(jnp.float32) + left.astype(jnp.float32)
    total = total.astype(jnp.bfloat16)
    return total


def row_sum(part, n):
    total = part.astype(jnp.float32)
    for step in range(1, n):
        other = lax.ppermute(part, "row", [(r, (r + step) % n) for r in range(n)])
        total = total + other.astype(jnp.float32)
    return total


def depth_masks(n):
    masks, bit = [0], n // 2
    while bit > 1:
        masks = masks + [m ^ bit for m in masks]
        bit //= 2
    return masks


def depth_high(mine, n):
    blocks, bit = [mine], n // 2
    while bit > 1:
        blocks = blocks + [
            lax.ppermute(b, "depth", [(d, d ^ bit) for d in range(n)]) for b in blocks
        ]
        bit //= 2
    return blocks


def high_columns(mine, masks, n):
    me = lax.axis_index("depth")
    width = 2 * mine.shape[1] // n
    out = []
    for m in masks:
        piece = lax.dynamic_slice_in_dim(mine, ((me ^ m) // 2) * width, width, axis=1)
        if m:
            piece = lax.ppermute(piece, "depth", [(d, d ^ m) for d in range(n)])
        out.append(piece)
    return out


def core_exchange(high, n):
    core = lax.axis_index("depth") % 2
    width = high.shape[1] // 2
    mine = lax.dynamic_slice_in_dim(high, core * width, width, axis=1)
    other = lax.dynamic_slice_in_dim(high, (1 - core) * width, width, axis=1)
    other = lax.ppermute(other, "depth", [(d, d ^ 1) for d in range(n)])
    first = core == 0
    return cat(jnp.where(first, mine, other), jnp.where(first, other, mine))


def core_gather(high, n):
    pairs = [[d, d + 1] for d in range(0, n, 2)]
    return lax.all_gather(high, "depth", axis=0, tiled=True, axis_index_groups=pairs)


def cat(*blocks):
    return jnp.concatenate(blocks, axis=0)


def body(n_row, n_col, n_depth, tokens, w_in, w_out, grad_out):
    rows = tokens.shape[0]
    tie = lax.optimization_barrier

    def fold(slots):
        return cat(*slots[0::2]), cat(*slots[1::2])

    def slot_of(held):
        def slot(k):
            return held["odd" if k % 2 else "even"][k // 2 * rows : (k // 2 + 1) * rows]

        return slot

    def own_part(part):
        return part.astype(jnp.bfloat16)

    step_high = lambda block: depth_high(block, n_depth)
    masks = depth_masks(n_depth)

    tok_slots, tok_high = line_gather(
        tokens,
        n_col,
        [lambda slot: step_high(tokens), lambda slot: step_high(grad_out), lambda slot: step_high(slot(2))],
    )
    tok_own, grad_own, tok_two = tok_high
    tok_even, tok_odd = fold(tok_slots)
    part_even = own_part(dot(tok_even, w_in, 1, 0))
    pre_even = row_sum(part_even, n_row)
    grad_out, tok_odd = tie((grad_out, tok_odd))
    tok_odd_high = step_high(tok_odd)
    tok_odd_in, _ = tie((tok_odd, part_even))
    part_odd = own_part(dot(tok_odd_in, w_in, 1, 0))
    pre_odd = row_sum(part_odd, n_row)
    grad_slots, grad_high = line_gather(
        grad_out, n_col, [lambda slot: part_odd, lambda slot: (pre_even, tok_odd_high), lambda slot: step_high(slot(2))]
    )
    pre_even, tok_odd_high = grad_high[1]
    grad_two = grad_high[2]
    act_even, pull_even = jax.vjp(gelu_tanh, pre_even)
    act_odd, pull_odd = jax.vjp(gelu_tanh, pre_odd)
    act_even, act_odd = own_part(act_even), own_part(act_odd)
    grad_even, grad_odd = fold(grad_slots)
    grad_odd_high = step_high(grad_odd)

    out_even = own_part(dot(act_even, w_out, 1, 0))
    grad_odd_in, out_even = tie((grad_odd, out_even))
    gact_odd_part = own_part(dot(grad_odd_in, w_out, 1, 1))
    gact_odd = row_sum(gact_odd_part, n_row)
    act_odd, _ = tie((act_odd, gact_odd_part))
    out_odd = own_part(dot(act_odd, w_out, 1, 0))
    grad_even_in, out_odd = tie((grad_even, out_odd))
    gact_even_part = own_part(dot(grad_even_in, w_out, 1, 1))
    gact_even = row_sum(gact_even_part, n_row)
    held = {"gact_odd": gact_odd}

    def out_hook(right, left):
        right, left, held["gact_odd"] = tie((right, left, held["gact_odd"]))
        return right, left

    output = line_reduce(slot_of({"even": out_even, "odd": out_odd}), n_col, {1: out_hook})
    gact_odd = held["gact_odd"]
    gact_odd, grad_odd_high, _ = tie((gact_odd, grad_odd_high, gact_even_part))
    act_high = high_columns(cat(act_even, act_odd), masks, n_depth)

    gpre_odd = own_part(pull_odd(gact_odd)[0])
    gtok_odd = own_part(dot(gpre_odd, w_in, 1, 1))

    def high_rows(own, two, odd_high, even, odd):
        blocks = [even, odd]
        for k in range(1, len(masks)):
            blocks += [own[k], two[k], odd_high[k]]
        return cat(*blocks)

    all_tok = core_gather(high_rows(tok_own, tok_two, tok_odd_high, tok_even, tok_odd), n_depth)
    all_grad = core_gather(
        high_rows(grad_own, grad_two, grad_odd_high, grad_even, grad_odd), n_depth
    )
    gtok = {"odd": gtok_odd}
    odd_high = high_columns(gpre_odd, masks, n_depth)

    def first_hook(right, left):
        right, left, gact, act_all = tie((right, left, gact_even, act_high))
        gpre_even = own_part(pull_even(gact)[0])
        gtok["even"] = own_part(dot(gpre_even, w_in, 1, 1))
        gtok["even_high"] = high_columns(gpre_even, masks, n_depth)
        all_act = core_exchange(cat(*act_all), n_depth)
        gtok["w_out"] = own_part(dot(all_act, all_grad, 0, 0))
        return right, left

    def later_hook(right, left):
        right, left, gtok["w_out"] = tie((right, left, gtok["w_out"]))
        return right, left

    hooks = {1: first_hook, 2: later_hook}
    grad_tokens = line_reduce(slot_of(gtok), n_col, hooks)
    gpre_high = zip(gtok["even_high"], odd_high)
    all_gpre = core_exchange(cat(*[b for pair in gpre_high for b in pair]), n_depth)
    grad_w_in = own_part(dot(all_tok, all_gpre, 0, 0))
    return output, grad_tokens, grad_w_in, gtok["w_out"]


def solution(mesh):
    placed = (
        P(("col", "depth"), "row"),
        P("row", "col"),
        P("col", "row"),
        P(("col", "depth"), "row"),
    )
    sizes = tuple(mesh.shape[a] for a in ("row", "col", "depth"))
    return jax.shard_map(
        lambda *args: body(*sizes, *args),
        mesh=mesh,
        in_specs=placed,
        out_specs=(
            P(("col", "depth"), "row"),
            P(("col", "depth"), "row"),
            P("row", ("col", "depth")),
            P(("col", "depth"), "row"),
        ),
        check_vma=False,
    )
```
